512 devices in a mesh: section: 16 (over y_lo, x, core), expert: 32 (over z, y_hi).
Axes of the slice: x: 4, y: 4 (y_hi: 2, y_lo: 2; y = y_hi * 2 + y_lo), z: 16, core: 2. Of those that a mesh axis runs over, the one named last changes fastest.
Arguments:
- tokens: bfloat16 [65536, 2048], P(('section', 'expert')), may hold values from -6 to 6
- upstream: bfloat16 [65536, 2048], P(('section', 'expert')), may hold values from -0.75 to 0.75
- expert_ids: int32 [65536, 1], P(('section', 'expert')), may hold values from 0 to 3; in each aligned block of 128 rows (0 to 127, 128 to 255, ...) at most 36 rows name the same one
- combine: bfloat16 [65536, 1], P(('section', 'expert')), may hold values from 0.049804688 to 0.3984375
- w_gate_up: bfloat16 [16, 32, 2048, 256], P('section', 'expert'), may hold values from -0.125 to 0.125
- w_down: bfloat16 [16, 32, 128, 2048], P('section', 'expert'), may hold values from -0.1875 to 0.1875
Outputs:
- input_grad: bfloat16 [65536, 2048], P(('section', 'expert'))
- combine_grad: bfloat16 [65536, 1], P(('section', 'expert'))
- grad_gate_up: bfloat16 [16, 32, 2048, 256], P('section', 'expert')
- grad_down: bfloat16 [16, 32, 128, 2048], P('section', 'expert')
The draws below stay inside these ranges and needn't reach their ends.
Inputs may be any that keep to these rules, and one draw needn't show every extreme that they name: `expert_ids`: each row names one expert; within the rows of one device no expert is named more than 36 times, a bound that some block reaches.
All inputs are finite; a program needn't handle non-finite values.
Results may differ from the reference program's by a relative error of at most 0.0058.
Values may be sent and summed in bfloat16 or wider, within the bound.
No kernel may reach another device: no remote copies, remote signals or barrier semaphores. Data moves between devices by JAX's collectives and lax.ppermute only.
A program may use at most 128 MiB of HBM per device.

```python
import math
import jax
import jax.numpy as jnp
import numpy as np
from jax import lax

D = 2048
FF_DEV = 128
TOP = 1
EXPERTS = 4
TOK_DEV = 128
SPLIT = 8
FF = 1024
CAP = 36
ROWS = 65536
N_SECTION = 16
N_EXPERT = 32


def level_of(own_key, shape, shards, low, high):
    gain, own = 1.0, jax.random.fold_in(own_key, 6)
    for position, shards_of in shards:
        draws = jnp.exp(jax.random.uniform(jax.random.fold_in(own, position), (shards_of,), jnp.float32, low / len(shards), high / len(shards)))
        gain = gain * jnp.repeat(draws, shape[position] // shards_of).reshape([-1 if axis == position else 1 for axis in range(len(shape))])
    return gain


def assign_block(rng, own, number, rows, number_of, top, most, lean):
    ranking = jax.random.permutation(rng, number_of)
    packed, ordinary = shares(number_of, rows * top, most, lean, True), shares(number_of, rows * top, most, lean, False)
    places = jnp.arange(number_of)

    def named(lengths, turn):
        used = int((lengths > 0).sum())
        fixed = max(1, used // 4)
        passed = fixed + (places - fixed + turn * (used - fixed)) % max(1, number_of - fixed)
        return jnp.zeros((number_of,), jnp.int32).at[ranking[jnp.where(places < fixed, places, passed)]].set(jnp.asarray(lengths, jnp.int32))

    lengths = jnp.where(number % 4 == 0, named(packed, number // 4), named(ordinary, number - number // 4 - 1))
    mixed = jax.random.permutation(jax.random.fold_in(own, 3), number_of)
    source_of, taker = mixed[0:number_of // 2 * 2:2], mixed[1:number_of // 2 * 2:2]
    slack = jnp.minimum(lengths[source_of] - 1, most - lengths[taker]) // 2
    slack = jnp.where((source_of == ranking[0]) | (taker == ranking[0]) | (lengths[taker] == 0), 0, jnp.maximum(slack, 0))
    passed = jax.random.randint(jax.random.fold_in(own, 4), (number_of // 2,), 0, 1 << 20) % (slack + 1)
    lengths = lengths.at[source_of].add(-passed).at[taker].add(passed)
    members = jnp.searchsorted(jnp.cumsum(lengths), jnp.arange(rows * top), side="right").astype(jnp.int32)
    grid = members.reshape(top, rows).T
    grid = grid[jax.random.permutation(jax.random.fold_in(own, 1), rows)]
    turn = jax.random.randint(jax.random.fold_in(own, 2), (rows, 1), 0, top)
    return jnp.take_along_axis(grid, (jnp.arange(top)[None, :] + turn) % top, axis=1)


def shares(amount, total, limit, lean, full):
    loads = [(1 << 20) // math.isqrt(standing ** lean) + 1 for standing in range(1, amount + 1)]
    largest = limit if full else min(limit, max(-(-total // amount), total * loads[0] // sum(loads)))
    least = 1 if total - largest >= amount - 1 else 0
    holding, surplus = [largest] + [least] * (amount - 1), total - largest - least * (amount - 1)
    while surplus > 0:
        movable = [i for i in range(1, amount) if holding[i] < largest] or [i for i in range(1, amount) if holding[i] < limit]
        pool, budget = sum([loads[i] for i in movable]), surplus
        for i in movable:
            extra = min(limit - holding[i], max(1, budget * loads[i] // pool), surplus)
            holding[i] = holding[i] + extra
            surplus = surplus - extra
    return np.array(holding)


def normal_values(own_key, dims, spread, limit, pieces=(), kind=jnp.bfloat16):
    result = jax.random.normal(own_key, dims, jnp.float32) * spread
    if len(pieces) > 0:
        result = level_of(own_key, dims, pieces, -0.22, 0.18) * result
    return jnp.clip(result, min=-limit, max=limit).astype(kind)


def setup_inputs(seed: int = 0) -> dict:
    seeds = jax.random.split(jax.random.key(seed), 7)
    tokens = normal_values(seeds[0], (ROWS, D), 1.0, 6.0, ((0, 512),))
    upstream = normal_values(seeds[1], (ROWS, D), 0.125, 0.75, ((0, 512),))
    expert_ids_keys = jax.random.split(jax.random.fold_in(seeds[2], 1), ROWS // TOK_DEV)
    expert_ids_turns = jax.random.permutation(jax.random.fold_in(seeds[2], 3), ROWS // TOK_DEV)
    expert_ids = jax.vmap(lambda own, number: assign_block(jax.random.fold_in(seeds[2], 2), own, number, TOK_DEV, EXPERTS, TOP, CAP, 2))(expert_ids_keys, expert_ids_turns).reshape((ROWS, TOP))
    combine = jnp.clip(0.049804688 + 0.3486328 * jax.random.uniform(seeds[3], (ROWS, TOP), jnp.float32) ** level_of(seeds[3], (ROWS, TOP), ((0, 512),), -0.2, 0.2), 0.049804688, 0.3984375).astype(jnp.bfloat16)
    w_gate_up = normal_values(seeds[4], (N_SECTION, N_EXPERT, D, 2 * FF_DEV), D ** -0.5, 0.125, ((0, 16), (1, 32)))
    w_down = normal_values(seeds[5], (N_SECTION, N_EXPERT, FF_DEV, D), FF ** -0.5, 0.1875, ((0, 16), (1, 32)))
    return {"tokens": tokens, "upstream": upstream, "expert_ids": expert_ids, "combine": combine, "w_gate_up": w_gate_up, "w_down": w_down}


def slot_rows(ids):
    onehot = (ids[:, :, None] == jnp.arange(EXPERTS, dtype=jnp.int32)[None, None, :]).astype(jnp.int32)
    flat = onehot.reshape(TOK_DEV * TOP, EXPERTS)
    before = jnp.cumsum(flat, axis=0) - flat
    slot = jnp.sum(before * flat, axis=1).reshape(TOK_DEV, TOP)
    return (ids * CAP + slot).astype(jnp.int32)


def expert_backward(xs, gs, ps, wgu, wdown):
    gu = jnp.dot(xs, wgu, preferred_element_type=jnp.float32)
    gate = gu[:, :FF_DEV]
    upper = gu[:, FF_DEV:]
    sig = jax.nn.sigmoid(gate)
    act = gate * sig
    hid = act * upper
    raw = lax.dot_general(gs, wdown, (((1,), (1,)), ((), ())), preferred_element_type=jnp.float32)
    part_dp = jnp.sum(hid * raw, axis=1).astype(jnp.bfloat16)
    pcol = ps.astype(jnp.float32)[:, None]
    scaled = (pcol * gs.astype(jnp.float32)).astype(jnp.bfloat16)
    grad_down = lax.dot_general(hid.astype(jnp.bfloat16), scaled, (((0,), (0,)), ((), ())), preferred_element_type=jnp.float32).astype(jnp.bfloat16)
    dhid = pcol * raw
    dgate = dhid * upper * sig * (1.0 + gate * (1.0 - sig))
    dupper = dhid * act
    dgu = jnp.concatenate([dgate, dupper], axis=1).astype(jnp.bfloat16)
    grad_gu = lax.dot_general(xs, dgu, (((0,), (0,)), ((), ())), preferred_element_type=jnp.float32).astype(jnp.bfloat16)
    part_dx = lax.dot_general(dgu, wgu, (((1,), (1,)), ((), ())), preferred_element_type=jnp.float32).astype(jnp.bfloat16)
    return part_dx, part_dp, grad_gu, grad_down


def one_section(operands):
    xin, gin, ids, comb, wgu, wdown = operands
    rows = EXPERTS * CAP
    buffer_rows = N_EXPERT * CAP
    dest = jax.vmap(slot_rows)(ids)
    match = (dest[:, None, :, :] == jnp.arange(rows, dtype=jnp.int32)[None, :, None, None]).astype(jnp.float32)
    place = jnp.sum(match, axis=3)
    send_x = jnp.einsum('brt,btd->brd', place, xin.astype(jnp.float32)).astype(jnp.bfloat16)
    send_g = jnp.einsum('brt,btd->brd', place, gin.astype(jnp.float32)).astype(jnp.bfloat16)
    send_p = jnp.einsum('brtk,btk->br', match, comb.astype(jnp.float32)).astype(jnp.bfloat16)
    recv_x = send_x.reshape(N_EXPERT, EXPERTS, CAP, D).transpose(1, 0, 2, 3).reshape(EXPERTS, buffer_rows, D)
    recv_g = send_g.reshape(N_EXPERT, EXPERTS, CAP, D).transpose(1, 0, 2, 3).reshape(EXPERTS, buffer_rows, D)
    recv_p = send_p.reshape(N_EXPERT, EXPERTS, CAP).transpose(1, 0, 2).reshape(EXPERTS, buffer_rows)

    def one_slice(index):
        owner = (index // SPLIT).astype(jnp.int32)
        return expert_backward(recv_x[owner], recv_g[owner], recv_p[owner], wgu[index], wdown[index])

    part_dx, part_dp, grad_gu, grad_down = lax.map(one_slice, jnp.arange(N_EXPERT, dtype=jnp.int32))
    total_dx = jnp.sum(part_dx.astype(jnp.float32).reshape(EXPERTS, SPLIT, buffer_rows, D), axis=1)
    total_dp = jnp.sum(part_dp.astype(jnp.float32).reshape(EXPERTS, SPLIT, buffer_rows), axis=1)
    back_x = total_dx.reshape(EXPERTS, N_EXPERT, CAP, D).transpose(1, 0, 2, 3).reshape(N_EXPERT, rows, D)
    back_p = total_dp.reshape(EXPERTS, N_EXPERT, CAP).transpose(1, 0, 2).reshape(N_EXPERT, rows)
    moe = jnp.einsum('brt,brd->btd', place, back_x)
    input_grad = (gin.astype(jnp.float32) + moe).astype(jnp.bfloat16)
    combine_grad = jnp.einsum('brtk,br->btk', match, back_p).astype(jnp.bfloat16)
    return input_grad, combine_grad, grad_gu, grad_down


def reference(tokens, upstream, expert_ids, combine, w_gate_up, w_down):
    xin = tokens.reshape(N_SECTION, N_EXPERT, TOK_DEV, D)
    gin = jnp.roll(upstream.reshape(N_SECTION, N_EXPERT, TOK_DEV, D), -1, axis=0)
    ids = expert_ids.reshape(N_SECTION, N_EXPERT, TOK_DEV, TOP)
    comb = combine.reshape(N_SECTION, N_EXPERT, TOK_DEV, TOP)
    input_grad, combine_grad, grad_gu, grad_down = lax.map(one_section, (xin, gin, ids, comb, w_gate_up, w_down))
    return (input_grad.reshape(ROWS, D), combine_grad.reshape(ROWS, TOP), grad_gu, grad_down)
```

```python
import jax
import jax.numpy as jnp
from jax import lax
from jax.sharding import Mesh, PartitionSpec as P

EXPERTS = 4
SECTION = ("ylo", "x", "core")
AXES = ("ylo", "x", "core", "zb", "zo", "yh")
LINE = 4
BF = jnp.bfloat16
F32 = jnp.float32


def dot(a, b, ca, cb):
    return lax.dot_general(a, b, (((ca,), (cb,)), ((), ())), preferred_element_type=F32)


def right(a, step):
    return lax.ppermute(a, "zo", [(i, i + 1) for i in range(step - 1, LINE - 1)])


def left(a, step):
    return lax.ppermute(a, "zo", [(i + 1, i) for i in range(LINE - step)])


def back_of_right(a, step):
    return lax.ppermute(a, "zo", [(i + 1, i) for i in range(step - 1, LINE - 1)])


def back_of_left(a, step):
    return lax.ppermute(a, "zo", [(i, i + 1) for i in range(LINE - step)])


def across(a):
    return lax.ppermute(a, "yh", [(0, 1), (1, 0)])


def plus(*terms):
    total = terms[0].astype(F32)
    for term in terms[1:]:
        total = total + term.astype(F32)
    return total.astype(BF)


def spread(unit, zo):
    r1, l1 = right(unit, 1), left(unit, 1)
    g1 = jnp.where(zo >= 1, r1, l1)
    r2, l2 = right(r1, 2), left(l1, 2)
    g2 = jnp.where(zo == 0, l2, jnp.where(zo == 3, r2, l1))
    r3, l3 = right(r2, 3), left(l2, 3)
    g3 = jnp.where(zo == 0, l3, jnp.where(zo == 1, l2, jnp.where(zo == 2, r2, r3)))
    own = [unit, g1, g2, g3]
    return own + [across(g) for g in own]


def gather_back(groups, zo):
    own, other = groups[:4], groups[4:]
    total = [None] * 4
    for k in (3, 2, 1, 0):
        total[k] = plus(own[k], across(other[k]))
    unit, g1, g2, g3 = total
    zero = jnp.zeros_like(unit)
    r3, l3 = back_of_right(g3, 3), back_of_left(g3, 3)
    c2r = jnp.where(zo == 3, g2, g3)
    c2l = jnp.where(zo == 0, g2, g3)
    r2 = back_of_right(plus(c2r, r3), 2)
    l2 = back_of_left(plus(c2l, l3), 2)
    r1 = back_of_right(plus(g1, r2), 1)
    c1l = jnp.where(zo == 0, g1, g2)
    l1 = back_of_left(plus(c1l, l2), 1)
    return plus(unit, r1, l1)


def per_device(tokens, upstream, expert_ids, combine, w_gate_up, w_down):
    tok, width = tokens.shape
    capacity = tok * 9 // (8 * EXPERTS)
    rows = EXPERTS * capacity
    wgu = w_gate_up[0, 0]
    wdown = w_down[0, 0]
    hidden = wdown.shape[0]
    zo = lax.axis_index("zo")
    sections = lax.axis_size(SECTION)
    out_grad = lax.ppermute(
        upstream, SECTION, [(i, (i - 1) % sections) for i in range(sections)]
    )

    ids = expert_ids[:, 0]
    onehot = (ids[:, None] == jnp.arange(EXPERTS, dtype=jnp.int32)[None, :]).astype(F32)
    earlier = (jnp.arange(tok)[:, None] > jnp.arange(tok)[None, :]).astype(F32)
    before = dot(earlier, onehot, 1, 0)
    slot = jnp.sum(before * onehot, axis=1).astype(jnp.int32)
    dest = ids * capacity + slot
    place = (jnp.arange(rows, dtype=jnp.int32)[:, None] == dest[None, :]).astype(BF)

    weight = combine.astype(F32)
    scaled = (weight * out_grad.astype(F32)).astype(BF)

    def to_block(a):
        sent = dot(place, a, 1, 0).astype(BF).reshape(EXPERTS, capacity, width)
        return lax.all_to_all(sent, "zb", 0, 0, tiled=True).reshape(rows, width)

    xs = spread(to_block(tokens), zo)
    gs = spread(to_block(scaled), zo)

    hs, dgus, dxs = [], [], []
    for x, g in zip(xs, gs):
        gu = dot(x, wgu, 1, 0)
        gate, upper = gu[:, :hidden], gu[:, hidden:]
        sig = jax.nn.sigmoid(gate)
        act = gate * sig
        hid = act * upper
        draw = dot(g, wdown, 1, 1)
        dp = jnp.sum(hid * draw, axis=1, keepdims=True)
        dgate = draw * upper * sig * (1.0 + gate * (1.0 - sig))
        dupper = draw * act
        dgu = jnp.concatenate([dgate, dupper], axis=1).astype(BF)
        dx = dot(dgu, wgu, 1, 1).astype(BF)
        dxs.append(
            jnp.concatenate([dx, jnp.broadcast_to(dp.astype(BF), (rows, 128))], axis=1)
        )
        hs.append(hid.astype(BF))
        dgus.append(dgu)

    back = gather_back(dxs, zo).reshape(EXPERTS, capacity, width + 128)
    back = lax.all_to_all(back, "zb", 0, 0, tiled=True).reshape(rows, width + 128)
    moe = dot(place, back, 0, 0)
    input_grad = (out_grad.astype(F32) + moe[:, :width]).astype(BF)
    combine_grad = (moe[:, width : width + 1] / weight).astype(BF)

    x_all = jnp.concatenate(xs, axis=0)
    g_all = jnp.concatenate(gs, axis=0)
    grad_gu = dot(x_all, jnp.concatenate(dgus, axis=0), 0, 0).astype(BF)
    grad_down = dot(jnp.concatenate(hs, axis=0), g_all, 0, 0).astype(BF)
    return (input_grad, combine_grad, grad_gu[None, None], grad_down[None, None])


def solution(mesh):
    fine = Mesh(mesh.devices.reshape(2, 4, 2, 4, 4, 2), AXES)
    row = P(AXES, None)
    weights = P(SECTION, ("zb", "zo", "yh"), None, None)
    return jax.shard_map(
        per_device,
        mesh=fine,
        in_specs=(row, row, row, row, weights, weights),
        out_specs=(row, row, weights, weights),
        check_vma=False,
    )
```

```python
import jax
import jax.numpy as jnp
from jax import lax
from jax.sharding import Mesh, PartitionSpec as P

EXPERTS = 4
SECTION = ("ylo", "x", "core")
AXES = ("ylo", "x", "core", "zb", "zo", "yh")
LINE = 4
RING = 16
BF = jnp.bfloat16
F32 = jnp.float32


def dot(a, b, ca, cb):
    return lax.dot_general(a, b, (((ca,), (cb,)), ((), ())), preferred_element_type=F32)


def up(a):
    return lax.ppermute(a, ("zb", "zo"), [(i, (i + 1) % RING) for i in range(RING)])


def down(a):
    return lax.ppermute(a, ("zb", "zo"), [((i + 1) % RING, i) for i in range(RING)])


def opposite(a):
    return lax.ppermute(a, "zb", [(i, (i + 2) % EXPERTS) for i in range(EXPERTS)])


def line_up(a, first, last):
    return lax.ppermute(a, "zo", [(i, i + 1) for i in range(first, last)])


def line_down(a, first, last):
    return lax.ppermute(a, "zo", [(i + 1, i) for i in range(first, last)])


def across(a):
    return lax.ppermute(a, "yh", [(0, 1), (1, 0)])


def plus(*terms):
    total = terms[0].astype(F32)
    for term in terms[1:]:
        total = total + term.astype(F32)
    return total.astype(BF)


def per_device(tokens, upstream, expert_ids, combine, w_gate_up, w_down):
    tok, width = tokens.shape
    cap = tok * 9 // (8 * EXPERTS)
    pitch = cap + 4
    wgu = w_gate_up[0, 0]
    wdown = w_down[0, 0]
    hidden = wdown.shape[0]
    zb, zo, yh = lax.axis_index("zb"), lax.axis_index("zo"), lax.axis_index("yh")
    member = zo * 2 + yh
    sections = lax.axis_size(SECTION)
    out_grad = lax.ppermute(
        upstream, SECTION, [(i, (i - 1) % sections) for i in range(sections)]
    )

    ids = expert_ids[:, 0]
    onehot = (ids[:, None] == jnp.arange(EXPERTS, dtype=jnp.int32)[None, :]).astype(F32)
    earlier = (jnp.arange(tok)[:, None] > jnp.arange(tok)[None, :]).astype(F32)
    before = dot(earlier, onehot, 1, 0)
    slot = jnp.sum(before * onehot, axis=1).astype(jnp.int32)
    rel = (ids - zb) % EXPERTS
    weight = combine.astype(F32)
    scaled = (weight * out_grad.astype(F32)).astype(BF)

    pick_x = rel * (2 * cap) + slot
    picks = jnp.concatenate([pick_x, pick_x + cap])
    place = (
        jnp.arange(EXPERTS * 2 * cap, dtype=jnp.int32)[:, None] == picks[None, :]
    ).astype(BF)
    sent = dot(place, jnp.concatenate([tokens, scaled], axis=0), 1, 0).astype(BF)
    sent = sent.reshape(EXPERTS, 2 * cap, width)

    ups, downs = [None, up(sent[1])], [None, down(sent[3])]
    far = opposite(sent[2])
    unit = jnp.concatenate([sent[0], far], axis=0)
    for _ in range(6):
        ups.append(up(ups[-1]))
        downs.append(down(downs[-1]))
    r1, l1 = line_up(unit, 0, 3), line_down(unit, 0, 3)
    r2, l2 = line_up(r1, 1, 3), line_down(l1, 0, 2)
    r3, l3 = line_up(r2, 2, 3), line_down(l2, 0, 1)
    where = jnp.where
    first, last, low = zo == 0, zo == 3, zo <= 1
    t1 = where(first, l1, r1)
    t2 = where(first, l2, where(last, r2, l1))
    t3 = where(first, l3, where(zo == 1, l2, where(last, r3, r2)))
    s2 = where(low, ups[2], downs[2])
    s6 = where(low, downs[6], ups[6])
    s1 = where(first, ups[1], where(last, downs[1], ups[3]))
    s3 = where(first, ups[3], downs[3])
    s5 = where(last, ups[5], downs[5])
    s7 = where(first, downs[7], where(last, ups[7], ups[5]))
    groups = [
        jnp.concatenate([unit, s2], axis=0),
        jnp.concatenate([t1, s1, s3], axis=0),
        jnp.concatenate([t2, ups[4], downs[4]], axis=0),
        jnp.concatenate([t3, s5, s6], axis=0),
        s7,
    ]

    lane = jnp.arange(width, dtype=jnp.int32)
    mine = ((lane // 128) == member).astype(F32)

    def expert(rows):
        count = rows.shape[0] // (2 * cap)
        gu = dot(rows, wgu, 1, 0).reshape(count, 2 * cap, 2 * hidden)[:, :cap]
        draw = dot(rows, wdown, 1, 1).reshape(count, 2 * cap, hidden)[:, cap:]
        gate, upper = gu[:, :, :hidden], gu[:, :, hidden:]
        sig = jax.nn.sigmoid(gate)
        act = gate * sig
        hid = act * upper
        dp = jnp.sum(hid * draw, axis=2)
        dgate = draw * upper * sig * (1.0 + gate * (1.0 - sig))
        dupper = draw * act
        dgu = jnp.concatenate([dgate, dupper], axis=2).astype(BF)
        pads = lambda a, lo, hi: jnp.pad(a, ((0, 0), (lo, hi), (0, 0)))
        dx = dot(pads(dgu, 0, 4).reshape(count * pitch, 2 * hidden), wgu, 1, 1)
        dp = jnp.tile(jnp.pad(dp, ((0, 0), (0, 128 - cap))), (1, width // 128)) * mine
        dp = pads(dp[:, None, :], cap, 3).reshape(count * pitch, width)
        dx = (dx + dp).astype(BF)
        dgu = pads(dgu, 0, cap).reshape(count * 2 * cap, 2 * hidden)
        hid = pads(hid.astype(BF), cap, 0).reshape(count * 2 * cap, hidden)
        return dx, dgu, hid

    others = [across(g) for g in groups]
    own_dx, other_dx, dgus, hids = [], [], [], []
    for g, o in zip(groups, others):
        dx, dgu, hid = expert(g)
        own_dx.append(dx)
        dgus.append(dgu)
        hids.append(hid)
        dx, dgu, hid = expert(o)
        other_dx.append(dx)
        dgus.append(dgu)
        hids.append(hid)

    total = [None] * 5
    for k in (4, 3, 2, 1, 0):
        total[k] = plus(own_dx[k], across(other_dx[k]))
    part = lambda a, lo, hi: a[lo * pitch : hi * pitch]
    b_unit, b_s2 = part(total[0], 0, 2), part(total[0], 2, 3)
    b_t1, b_s1, b_s3 = part(total[1], 0, 2), part(total[1], 2, 3), part(total[1], 3, 4)
    b_t2, b_u4, b_d4 = part(total[2], 0, 2), part(total[2], 2, 3), part(total[2], 3, 4)
    b_t3, b_s5, b_s6 = part(total[3], 0, 2), part(total[3], 2, 3), part(total[3], 3, 4)
    b_s7 = total[4]
    zero = jnp.zeros((), BF)
    mid = (zo == 1) | (zo == 2)
    from_ups = [
        where(first, b_s1, zero),
        where(low, b_s2, zero),
        where(first, b_s3, where(last, zero, b_s1)),
        b_u4,
        where(last, b_s5, where(first, zero, b_s7)),
        where(low, zero, b_s6),
        where(last, b_s7, zero),
    ]
    from_downs = [
        where(last, b_s1, zero),
        where(low, zero, b_s2),
        where(first, zero, b_s3),
        b_d4,
        where(last, zero, b_s5),
        where(low, b_s6, zero),
        where(first, b_s7, zero),
    ]
    back_next, back_prev = down(from_ups[6]), up(from_downs[6])
    for k in (5, 4, 3, 2, 1, 0):
        back_next = down(plus(from_ups[k], back_next))
        back_prev = up(plus(from_downs[k], back_prev))
    q3, m3 = line_down(b_t3, 2, 3), line_up(b_t3, 0, 1)
    q2 = line_down(plus(where(last, b_t2, b_t3), q3), 1, 3)
    m2 = line_up(plus(where(first, b_t2, b_t3), m3), 0, 2)
    q1 = line_down(plus(b_t1, q2), 0, 3)
    m1 = line_up(plus(where(first, b_t1, b_t2), m2), 0, 3)
    back_unit = plus(b_unit, q1, m1)
    back_far = opposite(back_unit[pitch:])
    back = jnp.concatenate([back_unit[:pitch], back_next, back_far, back_prev], axis=0)

    put = (
        jnp.arange(EXPERTS * pitch, dtype=jnp.int32)[:, None]
        == (rel * pitch + slot)[None, :]
    ).astype(BF)
    moe = dot(put, back, 0, 0)
    input_grad = (out_grad.astype(F32) + moe).astype(BF)
    dp = back.reshape(EXPERTS, pitch, width)[:, cap, : 8 * 128].astype(F32)
    dp = jnp.sum(dp.reshape(EXPERTS, 8, 128), axis=1)
    pick = (rel[:, None] == jnp.arange(EXPERTS)[None, :])[:, :, None] & (
        slot[:, None] == jnp.arange(128)[None, :]
    )[:, None, :]
    dp = jnp.sum(jnp.where(pick, dp[None], 0.0), axis=(1, 2))
    combine_grad = (dp[:, None] / weight).astype(BF)

    rows = jnp.concatenate([a for pair in zip(groups, others) for a in pair], axis=0)
    grad_gu = dot(rows, jnp.concatenate(dgus, axis=0), 0, 0).astype(BF)
    grad_down = dot(jnp.concatenate(hids, axis=0), rows, 0, 0).astype(BF)
    return (input_grad, combine_grad, grad_gu[None, None], grad_down[None, None])


def solution(mesh):
    fine = Mesh(mesh.devices.reshape(2, 4, 2, 4, 4, 2), AXES)
    row = P(AXES, None)
    weights = P(SECTION, ("zb", "zo", "yh"), None, None)
    return jax.shard_map(
        per_device,
        mesh=fine,
        in_specs=(row, row, row, row, weights, weights),
        out_specs=(row, row, weights, weights),
        check_vma=False,
    )
```

```python
import jax
import jax.numpy as jnp
from jax import lax
from jax.sharding import Mesh, PartitionSpec as P

EXPERTS = 4
SECTION = ("ylo", "x", "core")
AXES = ("ylo", "x", "core", "zb", "zo", "yh")
RING = 16
LINE = 4
BF = jnp.bfloat16
F32 = jnp.float32


def dot(a, b, ca, cb):
    return lax.dot_general(a, b, (((ca,), (cb,)), ((), ())), preferred_element_type=F32)


def up(a):
    return lax.ppermute(a, ("zb", "zo"), [(i, (i + 1) % RING) for i in range(RING)])


def down(a):
    return lax.ppermute(a, ("zb", "zo"), [((i + 1) % RING, i) for i in range(RING)])


def across(a):
    return lax.ppermute(a, "yh", [(0, 1), (1, 0)])


def after(a, *others):
    return lax.optimization_barrier((a, *others))[0]


def per_device(tokens, upstream, expert_ids, combine, w_gate_up, w_down):
    tok, width = tokens.shape
    cap = tok * 9 // (8 * EXPERTS)
    pitch = cap + 4
    wgu = w_gate_up[0, 0]
    wdown = w_down[0, 0]
    hidden = wdown.shape[0]
    zo = lax.axis_index("zo")
    sections = lax.axis_size(SECTION)
    out_grad = lax.ppermute(
        upstream, SECTION, [(i, (i - 1) % sections) for i in range(sections)]
    )

    ids = expert_ids[:, 0]
    onehot = (ids[:, None] == jnp.arange(EXPERTS, dtype=jnp.int32)[None, :]).astype(F32)
    earlier = (jnp.arange(tok)[:, None] > jnp.arange(tok)[None, :]).astype(F32)
    before = dot(earlier, onehot, 1, 0)
    slot = jnp.sum(before * onehot, axis=1).astype(jnp.int32)
    weight = combine.astype(F32)
    scaled = (weight * out_grad.astype(F32)).astype(BF)
    place = (
        jnp.arange(EXPERTS * cap, dtype=jnp.int32)[:, None]
        == (ids * cap + slot)[None, :]
    ).astype(BF)

    def to_blocks(a):
        sent = dot(place, a, 1, 0).astype(BF).reshape(EXPERTS, cap, width)
        unit = lax.all_to_all(sent, "zb", 0, 0, tiled=True)
        return unit.reshape(EXPERTS * cap, width)

    where = jnp.where
    first, last = zo == 0, zo == 3

    def relay(unit):
        r1, l1 = up(unit), down(unit)
        t1 = where(first, l1, r1)
        r2, l2 = up(r1), down(l1)
        t2 = where(first, l2, where(last, r2, l1))
        r3, l3 = up(r2), down(l2)
        t3 = where(first, l3, where(last, r3, where(zo == 1, l2, r2)))
        return [unit, t1, t2, t3]

    xs = relay(to_blocks(tokens))
    gs = relay(to_blocks(scaled))

    wgu_all = jnp.concatenate([wgu, across(after(wgu, xs[0]))], axis=1)
    wdown_all = jnp.concatenate([wdown, across(after(wdown, xs[0]))], axis=0)

    rows = EXPERTS * cap
    lane = jnp.arange(width, dtype=jnp.int32)
    mine = ((lane // 128) == zo).astype(F32)

    def forward(x):
        gu = dot(x, wgu_all, 1, 0).reshape(rows, 2, 2 * hidden)
        return gu[:, :, :hidden].reshape(rows, -1), gu[:, :, hidden:].reshape(rows, -1)

    def expert(gate, upper, g):
        draw = dot(g, wdown_all, 1, 1)
        sig = jax.nn.sigmoid(gate)
        act = gate * sig
        hid = act * upper
        dp = jnp.sum(hid * draw, axis=1)
        dgate = draw * upper * sig * (1.0 + gate * (1.0 - sig))
        dupper = draw * act
        split = lambda a: a.reshape(rows, 2, hidden)
        dgu = jnp.concatenate([split(dgate), split(dupper)], axis=2).astype(BF)
        return dgu.reshape(rows, 4 * hidden), hid.astype(BF), dp

    late = gs[1:] + [gs[3]]
    gus = [forward(after(x, l)) for x, l in zip(xs, (xs[1], xs[2], xs[3], xs[3]))]
    done = [expert(*gu, after(g, l)) for gu, g, l in zip(gus, gs, late)]
    dgus = jnp.stack([d[0] for d in done])

    order = jnp.array([[0, 1, 2, 3], [1, 0, 2, 3], [3, 1, 0, 2], [3, 2, 1, 0]])[zo]
    pads = lambda a: jnp.pad(
        a.reshape(LINE, EXPERTS, cap, -1), ((0, 0), (0, 0), (0, 4), (0, 0))
    )
    sorted_dgu = pads(dgus[order]).reshape(LINE * EXPERTS * pitch, 4 * hidden)
    dps = jnp.stack([d[2] for d in done])[order].reshape(LINE, EXPERTS, cap)
    dps = jnp.pad(dps, ((0, 0), (0, 0), (0, 128 - cap)))
    dps = jnp.tile(dps, (1, 1, width // 128)) * mine
    dps = jnp.pad(dps[:, :, None, :], ((0, 0), (0, 0), (cap, 3), (0, 0)))
    dx = dot(sorted_dgu, wgu_all, 1, 1) + dps.reshape(-1, width)
    dx = dx.astype(BF).reshape(LINE, EXPERTS * pitch, width)

    dx = lax.all_to_all(dx, "zo", 0, 0, tiled=True)
    dx = jnp.sum(dx.astype(F32), axis=0).astype(BF).reshape(EXPERTS, pitch, width)
    back = lax.all_to_all(dx, "zb", 0, 0, tiled=True).reshape(-1, width)

    put = (
        jnp.arange(EXPERTS * pitch, dtype=jnp.int32)[:, None]
        == (ids * pitch + slot)[None, :]
    ).astype(BF)
    moe = dot(put, back, 0, 0)
    input_grad = (out_grad.astype(F32) + moe).astype(BF)
    dp = back.reshape(EXPERTS, pitch, width)[:, cap, : LINE * 128].astype(F32)
    dp = jnp.sum(dp.reshape(EXPERTS, LINE, 128), axis=1)
    pick = (ids[:, None] == jnp.arange(EXPERTS)[None, :])[:, :, None] & (
        slot[:, None] == jnp.arange(128)[None, :]
    )[:, None, :]
    dp = jnp.sum(jnp.where(pick, dp[None], 0.0), axis=(1, 2))
    combine_grad = (dp[:, None] / weight).astype(BF)

    x_all = jnp.concatenate(xs, axis=0)
    g_all = jnp.concatenate(gs, axis=0)
    dgu_all = dgus.reshape(LINE * rows, 4 * hidden)
    hid_all = jnp.concatenate([d[1] for d in done], axis=0)
    other_gu = dot(x_all, dgu_all[:, 2 * hidden :], 0, 0).astype(BF)
    other_down = dot(hid_all[:, hidden:], g_all, 0, 0).astype(BF)
    other_gu, other_down = across(other_gu), across(other_down)
    grad_gu = dot(x_all, dgu_all[:, : 2 * hidden], 0, 0) + other_gu.astype(F32)
    grad_down = dot(hid_all[:, :hidden], g_all, 0, 0) + other_down.astype(F32)
    grad_gu, grad_down = grad_gu.astype(BF), grad_down.astype(BF)
    return (input_grad, combine_grad, grad_gu[None, None], grad_down[None, None])


def solution(mesh):
    fine = Mesh(mesh.devices.reshape(2, 4, 2, 4, 4, 2), AXES)
    row = P(AXES, None)
    weights = P(SECTION, ("zb", "zo", "yh"), None, None)
    return jax.shard_map(
        per_device,
        mesh=fine,
        in_specs=(row, row, row, row, weights, weights),
        out_specs=(row, row, weights, weights),
        check_vma=False,
    )
```

```python
import functools

import jax
import jax.numpy as jnp
from jax import lax
from jax.experimental import pallas as pl
from jax.experimental.pallas import tpu as pltpu
from jax.sharding import Mesh, PartitionSpec as P

EXPERTS = 4
SECTION = ("ylo", "x", "core")
AXES = ("ylo", "x", "core", "zb", "zo", "yh")
RING = 16
LINE = 4
LANES = 256
BF = jnp.bfloat16
F32 = jnp.float32


def dot(a, b, ca, cb):
    return lax.dot_general(a, b, (((ca,), (cb,)), ((), ())), preferred_element_type=F32)


def up(a):
    return lax.ppermute(a, ("zb", "zo"), [(i, (i + 1) % RING) for i in range(RING)])


def down(a):
    return lax.ppermute(a, ("zb", "zo"), [((i + 1) % RING, i) for i in range(RING)])


def line(a, *pairs):
    return lax.ppermute(a, "zo", pairs)


def across(a):
    return lax.ppermute(a, "yh", [(0, 1), (1, 0)])


def after(a, *others):
    return lax.optimization_barrier((a, *others))[0]


def slice_kernel(cap, zo_ref, gu_ref, g_ref, w_ref, wd_ref, own_ref, other_ref, h_ref, dx_ref):
    rows, hid2 = h_ref.shape
    hidden = hid2 // 2
    padded, width = dx_ref.shape
    pitch = padded // EXPERTS
    gate, upper = gu_ref[:, :hid2], gu_ref[:, hid2:]
    draw = dot(g_ref[...], wd_ref[...], 1, 1)
    sig = jax.nn.sigmoid(gate)
    act = gate * sig
    hid = act * upper
    h_ref[...] = hid.astype(BF)
    dgate = (draw * upper * sig * (1.0 + gate * (1.0 - sig))).astype(BF)
    dupper = (draw * act).astype(BF)
    own_ref[:, :hidden] = dgate[:, :hidden]
    own_ref[:, hidden:] = dupper[:, :hidden]
    other_ref[:, :hidden] = dgate[:, hidden:]
    other_ref[:, hidden:] = dupper[:, hidden:]
    to = lax.broadcasted_iota(jnp.int32, (padded, rows), 0)
    of = lax.broadcasted_iota(jnp.int32, (padded, rows), 1)
    pick = ((to // pitch * cap + to % pitch == of) & (to % pitch < cap)).astype(BF)
    dgu = jnp.concatenate([dgate, dupper], axis=1)
    dgu = dot(pick, dgu, 1, 0).astype(BF)
    dx = dot(dgu, w_ref[...], 1, 1)
    line = lax.dot_general(
        jnp.ones((8, hid2), F32),
        hid * draw,
        (((1,), (1,)), ((), ())),
        preferred_element_type=F32,
        precision=lax.Precision.HIGHEST,
    )
    line = jnp.concatenate([line, jnp.zeros((8, LANES - rows), F32)], axis=1)
    line = jnp.concatenate([line] * (width // LANES), axis=1)[:1]
    lane = lax.broadcasted_iota(jnp.int32, (1, width), 1)
    line = jnp.where(lane // LANES == zo_ref[0], line, 0.0)
    row = lax.broadcasted_iota(jnp.int32, (padded, width), 0)
    dx_ref[...] = jnp.where(row % pitch == cap, line, dx).astype(BF)


def slice_backward(cap, zo, gu, g, w, wd):
    rows, width = g.shape
    hid2 = wd.shape[0]
    whole = pl.BlockSpec(memory_space=pltpu.VMEM)
    return pl.pallas_call(
        functools.partial(slice_kernel, cap),
        out_shape=(
            jax.ShapeDtypeStruct((rows, hid2), BF),
            jax.ShapeDtypeStruct((rows, hid2), BF),
            jax.ShapeDtypeStruct((rows, hid2), BF),
            jax.ShapeDtypeStruct((EXPERTS * (cap + 4), width), BF),
        ),
        in_specs=[pl.BlockSpec(memory_space=pltpu.SMEM)] + [whole] * 4,
        out_specs=(whole,) * 4,
        compiler_params=pltpu.CompilerParams(vmem_limit_bytes=32 * 2**20),
        cost_estimate=pl.CostEstimate(
            flops=2 * rows * width * 3 * hid2, bytes_accessed=5 * 2**20, transcendentals=0
        ),
    )(zo, gu, g, w, wd)


def per_device(tokens, upstream, expert_ids, combine, w_gate_up, w_down):
    tok, width = tokens.shape
    cap = tok * 9 // (8 * EXPERTS)
    pitch = cap + 4
    wgu = w_gate_up[0, 0]
    wdown = w_down[0, 0]
    hidden = wdown.shape[0]
    zb, zo = lax.axis_index("zb"), lax.axis_index("zo")
    sections = lax.axis_size(SECTION)
    out_grad = lax.ppermute(
        upstream, SECTION, [(i, (i - 1) % sections) for i in range(sections)]
    )

    ids = expert_ids[:, 0]
    onehot = (ids[:, None] == jnp.arange(EXPERTS, dtype=jnp.int32)[None, :]).astype(F32)
    earlier = (jnp.arange(tok)[:, None] > jnp.arange(tok)[None, :]).astype(F32)
    before = dot(earlier, onehot, 1, 0)
    slot = jnp.sum(before * onehot, axis=1).astype(jnp.int32)
    weight = combine.astype(F32)
    scaled = (weight * out_grad.astype(F32)).astype(BF)
    place = (
        jnp.arange(EXPERTS * cap, dtype=jnp.int32)[:, None]
        == (ids * cap + slot)[None, :]
    ).astype(BF)

    def to_blocks(a):
        sent = dot(place, a, 1, 0).astype(BF).reshape(EXPERTS, cap, width)
        unit = lax.all_to_all(sent, "zb", 0, 0, tiled=True)
        return unit.reshape(EXPERTS * cap, width)

    where = jnp.where
    first, last, odd = zo == 0, zo == 3, (zo % 2) == 1

    def relay(unit):
        r1, l1 = up(unit), down(unit)
        r2, l2 = up(r1), down(l1)
        r3, l3 = line(r2, (2, 3)), line(l2, (1, 0))
        early = where(odd, l1, r1)
        whole = lambda *others: where(
            first, after(l3, *others), where(last, after(r3, *others), early)
        )
        return [unit, where(odd, r1, l1), early, where(zo < 2, l2, r2)], whole

    unit_x = to_blocks(tokens)
    unit_g = to_blocks(scaled)
    wgu_other, wdown_other = across(wgu), across(wdown)
    unit_x, wgu_other = lax.optimization_barrier((unit_x, wgu_other))
    unit_g, wdown_other = lax.optimization_barrier((unit_g, wdown_other))
    parts = [a[:, k : k + hidden] for k in (0, hidden) for a in (wgu, wgu_other)]
    wgu_all = jnp.concatenate(parts, axis=1)
    wdown_all = jnp.concatenate([wdown, wdown_other], axis=0)
    (xs, x3), (gs, g3) = relay(unit_x), relay(unit_g)

    forward = lambda x: dot(x, wgu_all, 1, 0)
    expert = lambda gu, g: slice_backward(cap, zo[None], gu, g, wgu_all, wdown_all)
    gus = [forward(after(xs[k], xs[l])) for k, l in ((0, 1), (1, 3), (2, 3))]
    x3 = x3(*gus)
    gus.append(forward(after(xs[3], gs[1])))
    gu3 = forward(x3)
    early = (xs[3], xs[3], xs[3], gs[3])
    done = [expert(gu, after(g, e)) for gu, g, e in zip(gus, gs, early)]

    add = lambda *terms: sum(a.astype(F32) for a in terms).astype(BF)
    d0, d1, d3_early, d2 = (d[3] for d in done)
    near = line(d1, (0, 1), (3, 2))
    r2, l2 = line(d2, (0, 1), (1, 2)), line(d2, (3, 2), (2, 1))
    to_r1 = add(where(zo == 1, d3_early, d1), r2)
    to_l1 = add(where(zo == 2, d3_early, d1), l2)
    r1, l1 = line(to_r1, (1, 2), (2, 3)), line(to_l1, (2, 1), (1, 0))
    g3 = g3(to_r1, to_l1, gu3)
    done[2] = expert(gu3, g3)
    far = line(done[2][3], (0, 3), (3, 0))
    own, other, hids, _ = zip(*(done[k] for k in (0, 1, 3, 2)))

    cat = lambda arrays: jnp.concatenate(arrays, axis=0)
    x_all, g_all = cat([xs[0], xs[1], xs[3], x3]), cat([gs[0], gs[1], gs[3], g3])
    hid_all = cat(hids)
    other_gu = dot(x_all, cat(other), 0, 0).astype(BF)
    other_down = dot(hid_all[:, hidden:], g_all, 0, 0).astype(BF)

    dx = add(d0, near, r1, l1, after(far, other_gu, other_down))
    dx = dx.reshape(EXPERTS, pitch, width)
    back = lax.all_to_all(dx, "zb", 0, 0, tiled=True).reshape(-1, width)
    other_gu, other_down = across(other_gu), across(other_down)
    grad_gu = (dot(x_all, cat(own), 0, 0) + other_gu.astype(F32)).astype(BF)
    grad_down = dot(hid_all[:, :hidden], g_all, 0, 0) + other_down.astype(F32)
    grad_down = grad_down.astype(BF)
    back, grad_gu, grad_down = lax.optimization_barrier((back, grad_gu, grad_down))

    put = (
        jnp.arange(EXPERTS * pitch, dtype=jnp.int32)[:, None]
        == (ids * pitch + slot)[None, :]
    ).astype(BF)
    moe = dot(put, back, 0, 0)
    input_grad = (out_grad.astype(F32) + moe).astype(BF)
    dp = back.reshape(EXPERTS, pitch, width)[:, cap, : LINE * LANES].astype(F32)
    dp = jnp.sum(dp.reshape(EXPERTS, LINE, LANES), axis=1)
    pick = (ids[:, None] == jnp.arange(EXPERTS)[None, :])[:, :, None] & (
        (zb * cap + slot)[:, None] == jnp.arange(LANES)[None, :]
    )[:, None, :]
    dp = jnp.sum(jnp.where(pick, dp[None], 0.0), axis=(1, 2))
    combine_grad = (dp[:, None] / weight).astype(BF)

    return (input_grad, combine_grad, grad_gu[None, None], grad_down[None, None])


def solution(mesh):
    fine = Mesh(mesh.devices.reshape(2, 4, 2, 4, 4, 2), AXES)
    row = P(AXES, None)
    weights = P(SECTION, ("zb", "zo", "yh"), None, None)
    return jax.shard_map(
        per_device,
        mesh=fine,
        in_specs=(row, row, row, row, weights, weights),
        out_specs=(row, row, weights, weights),
        check_vma=False,
    )
```

```python
import functools

import jax
import jax.numpy as jnp
from jax import lax
from jax.experimental import pallas as pl
from jax.experimental.pallas import tpu as pltpu
from jax.sharding import Mesh, PartitionSpec as P

EXPERTS = 4
SECTION = ("ylo", "x", "core")
AXES = ("ylo", "x", "core", "zb", "zo", "yh")
RING = 16
LINE = 4
LANES = 256
BF = jnp.bfloat16
F32 = jnp.float32


def dot(a, b, ca, cb):
    return lax.dot_general(a, b, (((ca,), (cb,)), ((), ())), preferred_element_type=F32)


def up(a):
    return lax.ppermute(a, ("zb", "zo"), [(i, (i + 1) % RING) for i in range(RING)])


def down(a):
    return lax.ppermute(a, ("zb", "zo"), [((i + 1) % RING, i) for i in range(RING)])


def line(a, *pairs):
    return lax.ppermute(a, "zo", pairs)


def across(a):
    return lax.ppermute(a, "yh", [(0, 1), (1, 0)])


def after(a, *others):
    return lax.optimization_barrier((a, *others))[0]


def slice_kernel(cap, zo_ref, gu_ref, g_ref, w_ref, wd_ref, own_ref, other_ref, h_ref, dx_ref):
    rows, hid2 = h_ref.shape
    hidden = hid2 // 2
    padded, width = dx_ref.shape
    pitch = padded // EXPERTS
    gate, upper = gu_ref[:, :hid2], gu_ref[:, hid2:]
    draw = dot(g_ref[...], wd_ref[...], 1, 1)
    sig = jax.nn.sigmoid(gate)
    act = gate * sig
    hid = act * upper
    h_ref[...] = hid.astype(BF)
    dgate = (draw * upper * sig * (1.0 + gate * (1.0 - sig))).astype(BF)
    dupper = (draw * act).astype(BF)
    own_ref[:, :hidden] = dgate[:, :hidden]
    own_ref[:, hidden:] = dupper[:, :hidden]
    other_ref[:, :hidden] = dgate[:, hidden:]
    other_ref[:, hidden:] = dupper[:, hidden:]
    to = lax.broadcasted_iota(jnp.int32, (padded, rows), 0)
    of = lax.broadcasted_iota(jnp.int32, (padded, rows), 1)
    pick = ((to // pitch * cap + to % pitch == of) & (to % pitch < cap)).astype(BF)
    dgu = jnp.concatenate([dgate, dupper], axis=1)
    dgu = dot(pick, dgu, 1, 0).astype(BF)
    dx = dot(dgu, w_ref[...], 1, 1)
    line = lax.dot_general(
        jnp.ones((8, hid2), F32),
        hid * draw,
        (((1,), (1,)), ((), ())),
        preferred_element_type=F32,
        precision=lax.Precision.HIGHEST,
    )
    line = jnp.concatenate([line, jnp.zeros((8, LANES - rows), F32)], axis=1)
    line = jnp.concatenate([line] * (width // LANES), axis=1)[:1]
    lane = lax.broadcasted_iota(jnp.int32, (1, width), 1)
    line = jnp.where(lane // LANES == zo_ref[0], line, 0.0)
    row = lax.broadcasted_iota(jnp.int32, (padded, width), 0)
    dx_ref[...] = jnp.where(row % pitch == cap, line, dx).astype(BF)


def slice_backward(cap, zo, gu, g, w, wd):
    rows, width = g.shape
    hid2 = wd.shape[0]
    whole = pl.BlockSpec(memory_space=pltpu.VMEM)
    return pl.pallas_call(
        functools.partial(slice_kernel, cap),
        out_shape=(
            jax.ShapeDtypeStruct((rows, hid2), BF),
            jax.ShapeDtypeStruct((rows, hid2), BF),
            jax.ShapeDtypeStruct((rows, hid2), BF),
            jax.ShapeDtypeStruct((EXPERTS * (cap + 4), width), BF),
        ),
        in_specs=[pl.BlockSpec(memory_space=pltpu.SMEM)] + [whole] * 4,
        out_specs=(whole,) * 4,
        compiler_params=pltpu.CompilerParams(vmem_limit_bytes=32 * 2**20),
        cost_estimate=pl.CostEstimate(
            flops=2 * rows * width * 3 * hid2, bytes_accessed=5 * 2**20, transcendentals=0
        ),
    )(zo, gu, g, w, wd)


def per_device(tokens, upstream, expert_ids, combine, w_gate_up, w_down):
    tok, width = tokens.shape
    cap = tok * 9 // (8 * EXPERTS)
    pitch = cap + 4
    wgu = w_gate_up[0, 0]
    wdown = w_down[0, 0]
    hidden = wdown.shape[0]
    zb, zo = lax.axis_index("zb"), lax.axis_index("zo")
    sections = lax.axis_size(SECTION)
    out_grad = lax.ppermute(
        upstream, SECTION, [(i, (i - 1) % sections) for i in range(sections)]
    )

    ids = expert_ids[:, 0]
    onehot = (ids[:, None] == jnp.arange(EXPERTS, dtype=jnp.int32)[None, :]).astype(F32)
    earlier = (jnp.arange(tok)[:, None] > jnp.arange(tok)[None, :]).astype(F32)
    before = dot(earlier, onehot, 1, 0)
    slot = jnp.sum(before * onehot, axis=1).astype(jnp.int32)
    rel = (ids - zb) % EXPERTS
    weight = combine.astype(F32)
    scaled = (weight * out_grad.astype(F32)).astype(BF)
    place = (
        jnp.arange(EXPERTS * cap, dtype=jnp.int32)[:, None]
        == (ids * cap + slot)[None, :]
    ).astype(BF)

    def dispatch(a):
        return dot(place, a, 1, 0).astype(BF).reshape(EXPERTS, cap, width)

    def block(a, k):
        return lax.ppermute(a, "zb", [(i, (i + k) % EXPERTS) for i in range(EXPERTS)])

    where = jnp.where
    first, last, odd = zo == 0, zo == 3, (zo % 2) == 1

    def relay(unit):
        r1, l1 = up(unit), down(unit)
        r2, l2 = up(r1), down(l1)
        r3, l3 = line(r2, (2, 3)), line(l2, (1, 0))
        early = where(odd, l1, r1)
        whole = lambda *others: where(
            first, after(l3, *others), where(last, after(r3, *others), early)
        )
        units = [unit, where(odd, r1, l1), early, where(zo < 2, l2, r2)]
        return units, whole

    from_block = (zb - jnp.arange(EXPERTS)) % EXPERTS

    def to_blocks(a):
        units = lax.all_to_all(dispatch(a), "zb", 0, 0, tiled=True)
        return units[from_block].reshape(-1, width)

    unit_x, unit_g = to_blocks(tokens), to_blocks(scaled)
    wgu_other, wdown_other = across(wgu), across(wdown)
    unit_x, wgu_other = lax.optimization_barrier((unit_x, wgu_other))
    unit_g, wdown_other = lax.optimization_barrier((unit_g, wdown_other))
    parts = [a[:, k : k + hidden] for k in (0, hidden) for a in (wgu, wgu_other)]
    wgu_all = jnp.concatenate(parts, axis=1)
    wdown_all = jnp.concatenate([wdown, wdown_other], axis=0)
    (xs, x3), (gs, g3) = relay(unit_x), relay(unit_g)

    forward = lambda x: dot(x, wgu_all, 1, 0)
    expert = lambda gu, g: slice_backward(cap, zo[None], gu, g, wgu_all, wdown_all)
    gus = [forward(after(xs[k], xs[l])) for k, l in ((0, 1), (1, 3), (2, 3))]
    x3 = x3(*gus)
    gus.append(forward(after(xs[3], gs[1])))
    gu3 = forward(x3)
    early = (x3, x3, x3, gs[3])
    done = [expert(gu, after(g, e)) for gu, g, e in zip(gus, gs, early)]

    add = lambda *terms: sum(a.astype(F32) for a in terms).astype(BF)
    d0, d1, d3_early, d2 = (d[3] for d in done)
    near = line(d1, (0, 1), (3, 2))
    r2, l2 = line(d2, (0, 1), (1, 2)), line(d2, (3, 2), (2, 1))
    to_r1 = add(where(zo == 1, d3_early, d1), r2)
    to_l1 = add(where(zo == 2, d3_early, d1), l2)
    r1, l1 = line(to_r1, (1, 2), (2, 3)), line(to_l1, (2, 1), (1, 0))
    g3 = g3(to_r1, to_l1, gu3)
    done[2] = expert(gu3, g3)
    far = line(done[2][3], (0, 3), (3, 0))
    own, other, hids, _ = zip(*(done[k] for k in (0, 1, 3, 2)))

    cat = lambda arrays: jnp.concatenate(arrays, axis=0)
    x_all, g_all = cat([xs[0], xs[1], xs[3], x3]), cat([gs[0], gs[1], gs[3], g3])
    hid_all = cat(hids)
    other_gu = dot(x_all, cat(other), 0, 0).astype(BF)
    other_down = dot(hid_all[:, hidden:], g_all, 0, 0).astype(BF)

    other_down = across(other_down)
    dx = add(d0, near, r1, l1, after(far, other_gu, other_down))
    dx = dx.reshape(EXPERTS, pitch, width)
    far, up1, down1 = (block(dx[k], -k) for k in (2, 1, 3))
    back = jnp.concatenate([dx[0], up1, far, down1], axis=0)
    other_gu = across(other_gu)
    grad_gu = (dot(x_all, cat(own), 0, 0) + other_gu.astype(F32)).astype(BF)
    grad_down = dot(hid_all[:, :hidden], g_all, 0, 0) + other_down.astype(F32)
    grad_down = grad_down.astype(BF)
    back, grad_gu, grad_down = lax.optimization_barrier((back, grad_gu, grad_down))

    put = (
        jnp.arange(EXPERTS * pitch, dtype=jnp.int32)[:, None]
        == (rel * pitch + slot)[None, :]
    ).astype(BF)
    moe = dot(put, back, 0, 0)
    input_grad = (out_grad.astype(F32) + moe).astype(BF)
    dp = back.reshape(EXPERTS, pitch, width)[:, cap, : LINE * LANES].astype(F32)
    dp = jnp.sum(dp.reshape(EXPERTS, LINE, LANES), axis=1)
    pick = (rel[:, None] == jnp.arange(EXPERTS)[None, :])[:, :, None] & (
        (rel * cap + slot)[:, None] == jnp.arange(LANES)[None, :]
    )[:, None, :]
    dp = jnp.sum(jnp.where(pick, dp[None], 0.0), axis=(1, 2))
    combine_grad = (dp[:, None] / weight).astype(BF)

    return (input_grad, combine_grad, grad_gu[None, None], grad_down[None, None])


def solution(mesh):
    fine = Mesh(mesh.devices.reshape(2, 4, 2, 4, 4, 2), AXES)
    row = P(AXES, None)
    weights = P(SECTION, ("zb", "zo", "yh"), None, None)
    return jax.shard_map(
        per_device,
        mesh=fine,
        in_specs=(row, row, row, row, weights, weights),
        out_specs=(row, row, weights, weights),
        check_vma=False,
    )
```

```python
import functools

import jax
import jax.numpy as jnp
from jax import lax
from jax.experimental import pallas as pl
from jax.experimental.pallas import tpu as pltpu
from jax.sharding import Mesh, PartitionSpec as P

EXPERTS = 4
SECTION = ("ylo", "x", "core")
AXES = ("ylo", "x", "core", "zb", "zo", "yh")
RING = 16
LINE = 4
LANES = 256
BF = jnp.bfloat16
F32 = jnp.float32


def dot(a, b, ca, cb):
    return lax.dot_general(a, b, (((ca,), (cb,)), ((), ())), preferred_element_type=F32)


def up(a):
    return lax.ppermute(a, ("zb", "zo"), [(i, (i + 1) % RING) for i in range(RING)])


def down(a):
    return lax.ppermute(a, ("zb", "zo"), [((i + 1) % RING, i) for i in range(RING)])


def line(a, *pairs):
    return lax.ppermute(a, "zo", pairs)


def across(a):
    return lax.ppermute(a, "yh", [(0, 1), (1, 0)])


def after(a, *others):
    return lax.optimization_barrier((a, *others))[0]


def slice_kernel(cap, at_ref, gu_ref, g_ref, w_ref, wd_ref, own_ref, other_ref, h_ref, dx_ref):
    rows, hid2 = h_ref.shape
    hidden = hid2 // 2
    padded, width = dx_ref.shape
    pitch = padded // EXPERTS
    gate, upper = gu_ref[:, :hid2], gu_ref[:, hid2:]
    draw = dot(g_ref[...], wd_ref[...], 1, 1)
    sig = jax.nn.sigmoid(gate)
    act = gate * sig
    hid = act * upper
    h_ref[...] = hid.astype(BF)
    dgate = (draw * upper * sig * (1.0 + gate * (1.0 - sig))).astype(BF)
    dupper = (draw * act).astype(BF)
    own_ref[:, :hidden] = dgate[:, :hidden]
    own_ref[:, hidden:] = dupper[:, :hidden]
    other_ref[:, :hidden] = dgate[:, hidden:]
    other_ref[:, hidden:] = dupper[:, hidden:]
    to = lax.broadcasted_iota(jnp.int32, (padded, rows), 0)
    of = lax.broadcasted_iota(jnp.int32, (padded, rows), 1)
    group = (at_ref[1] + EXPERTS - to // pitch) % EXPERTS
    pick = ((group * cap + to % pitch == of) & (to % pitch < cap)).astype(BF)
    dgu = jnp.concatenate([dgate, dupper], axis=1)
    dgu = dot(pick, dgu, 1, 0).astype(BF)
    dx = dot(dgu, w_ref[...], 1, 1)
    line = lax.dot_general(
        jnp.ones((8, hid2), F32),
        hid * draw,
        (((1,), (1,)), ((), ())),
        preferred_element_type=F32,
        precision=lax.Precision.HIGHEST,
    )
    line = jnp.concatenate([line, jnp.zeros((8, LANES - rows), F32)], axis=1)
    line = jnp.concatenate([line] * (width // LANES), axis=1)[:1]
    lane = lax.broadcasted_iota(jnp.int32, (1, width), 1)
    line = jnp.where(lane // LANES == at_ref[0], line, 0.0)
    row = lax.broadcasted_iota(jnp.int32, (padded, width), 0)
    dx_ref[...] = jnp.where(row % pitch == cap, line, dx).astype(BF)


def slice_backward(cap, at, gu, g, w, wd):
    rows, width = g.shape
    hid2 = wd.shape[0]
    whole = pl.BlockSpec(memory_space=pltpu.VMEM)
    return pl.pallas_call(
        functools.partial(slice_kernel, cap),
        out_shape=(
            jax.ShapeDtypeStruct((rows, hid2), BF),
            jax.ShapeDtypeStruct((rows, hid2), BF),
            jax.ShapeDtypeStruct((rows, hid2), BF),
            jax.ShapeDtypeStruct((EXPERTS * (cap + 4), width), BF),
        ),
        in_specs=[pl.BlockSpec(memory_space=pltpu.SMEM)] + [whole] * 4,
        out_specs=(whole,) * 4,
        compiler_params=pltpu.CompilerParams(vmem_limit_bytes=32 * 2**20),
        cost_estimate=pl.CostEstimate(
            flops=2 * rows * width * 3 * hid2, bytes_accessed=5 * 2**20, transcendentals=0
        ),
    )(at, gu, g, w, wd)


def per_device(tokens, upstream, expert_ids, combine, w_gate_up, w_down):
    tok, width = tokens.shape
    cap = tok * 9 // (8 * EXPERTS)
    pitch = cap + 4
    wgu = w_gate_up[0, 0]
    wdown = w_down[0, 0]
    hidden = wdown.shape[0]
    zb, zo = lax.axis_index("zb"), lax.axis_index("zo")
    sections = lax.axis_size(SECTION)
    out_grad = lax.ppermute(
        upstream, SECTION, [(i, (i - 1) % sections) for i in range(sections)]
    )

    ids = expert_ids[:, 0]
    onehot = (ids[:, None] == jnp.arange(EXPERTS, dtype=jnp.int32)[None, :]).astype(F32)
    earlier = (jnp.arange(tok)[:, None] > jnp.arange(tok)[None, :]).astype(F32)
    before = dot(earlier, onehot, 1, 0)
    slot = jnp.sum(before * onehot, axis=1).astype(jnp.int32)
    rel = (ids - zb) % EXPERTS
    weight = combine.astype(F32)
    scaled = (weight * out_grad.astype(F32)).astype(BF)
    row = jnp.arange(EXPERTS * cap, dtype=jnp.int32)[:, None]

    def dispatch(a, expert):
        place = (row == (expert * cap + slot)[None, :]).astype(BF)
        return dot(place, a, 1, 0).astype(BF).reshape(EXPERTS, cap, width)

    def block(a, k):
        return lax.ppermute(a, "zb", [(i, (i + k) % EXPERTS) for i in range(EXPERTS)])

    where = jnp.where
    first, last, odd = zo == 0, zo == 3, (zo % 2) == 1

    def relay(unit):
        r1, l1 = up(unit), down(unit)
        r2, l2 = up(r1), down(l1)
        r3, l3 = line(r2, (2, 3)), line(l2, (1, 0))
        early = where(odd, l1, r1)
        whole = lambda *others: where(
            first, after(l3, *others), where(last, after(r3, *others), early)
        )
        units = [unit, where(odd, r1, l1), early, where(zo < 2, l2, r2)]
        return units, whole

    unit_x = lax.all_to_all(dispatch(tokens, ids), "zb", 0, 0, tiled=True)
    unit_x = unit_x[(zb - jnp.arange(EXPERTS)) % EXPERTS].reshape(-1, width)
    sent = dispatch(scaled, rel)
    came = [block(sent[k], k) for k in (2, 1, 3)]
    g2, g1, g3, _ = lax.optimization_barrier((*came, unit_x))
    unit_g = jnp.concatenate([sent[0], g1, g2, g3], axis=0)
    wgu_other, wdown_other = across(wgu), across(wdown)
    unit_x, wgu_other = lax.optimization_barrier((unit_x, wgu_other))
    unit_g, wdown_other = lax.optimization_barrier((unit_g, wdown_other))
    parts = [a[:, k : k + hidden] for k in (0, hidden) for a in (wgu, wgu_other)]
    wgu_all = jnp.concatenate(parts, axis=1)
    wdown_all = jnp.concatenate([wdown, wdown_other], axis=0)
    (xs, x3), (gs, g3) = relay(unit_x), relay(unit_g)

    forward = lambda x: dot(x, wgu_all, 1, 0)
    at = jnp.stack([zo, zb]).astype(jnp.int32)
    expert = lambda gu, g: slice_backward(cap, at, gu, g, wgu_all, wdown_all)
    gus = [forward(after(xs[k], xs[l])) for k, l in ((0, 1), (1, 3), (2, 3))]
    x3 = x3(*gus)
    gus.append(forward(after(xs[3], gs[1])))
    gu3 = forward(x3)
    early = (x3, x3, x3, x3)
    done = [expert(gu, after(g, e)) for gu, g, e in zip(gus, gs, early)]

    add = lambda *terms: sum(a.astype(F32) for a in terms).astype(BF)
    d0, d1, d3_early, d2 = (d[3] for d in done)
    r2, l2 = line(d2, (0, 1), (1, 2)), line(d2, (3, 2), (2, 1))
    to_r1 = add(where(zo == 1, d3_early, d1), r2)
    to_l1 = add(where(zo == 2, d3_early, d1), l2)
    g3 = g3(gu3, d0, d2, d3_early)
    done[2] = expert(gu3, g3)
    far = line(done[2][3], (0, 3), (3, 0))
    to_r1, to_l1, _ = lax.optimization_barrier((to_r1, to_l1, done[2][3]))
    r1 = line(to_r1, (0, 1), (1, 2), (2, 3))
    l1 = line(to_l1, (3, 2), (2, 1), (1, 0))
    own, other, hids, _ = zip(*(done[k] for k in (0, 1, 3, 2)))

    cat = lambda arrays: jnp.concatenate(arrays, axis=0)
    x_all, g_all = cat([xs[0], xs[1], xs[3], x3]), cat([gs[0], gs[1], gs[3], g3])
    hid_all = cat(hids)
    other_gu = dot(x_all, cat(other), 0, 0).astype(BF)
    other_down = dot(hid_all[:, hidden:], g_all, 0, 0).astype(BF)

    other_down = across(other_down)
    dx = add(d0, r1, l1, after(far, other_gu, other_down)).reshape(EXPERTS, pitch, width)
    back = lax.all_to_all(dx, "zb", 0, 0, tiled=True).reshape(-1, width)
    other_gu = across(other_gu)
    own_gu = lax.optimization_barrier(dot(x_all, cat(own), 0, 0))
    grad_gu = (own_gu + other_gu.astype(F32)).astype(BF)
    grad_down = dot(hid_all[:, :hidden], g_all, 0, 0) + other_down.astype(F32)
    grad_down = grad_down.astype(BF)
    back, grad_gu, grad_down = lax.optimization_barrier((back, grad_gu, grad_down))

    put = (
        jnp.arange(EXPERTS * pitch, dtype=jnp.int32)[:, None]
        == (ids * pitch + slot)[None, :]
    ).astype(BF)
    moe = dot(put, back, 0, 0)
    input_grad = (out_grad.astype(F32) + moe).astype(BF)
    dp = back.reshape(EXPERTS, pitch, width)[:, cap, : LINE * LANES].astype(F32)
    dp = jnp.sum(dp.reshape(EXPERTS, LINE, LANES), axis=1)
    pick = (ids[:, None] == jnp.arange(EXPERTS)[None, :])[:, :, None] & (
        (rel * cap + slot)[:, None] == jnp.arange(LANES)[None, :]
    )[:, None, :]
    dp = jnp.sum(jnp.where(pick, dp[None], 0.0), axis=(1, 2))
    combine_grad = (dp[:, None] / weight).astype(BF)

    return (input_grad, combine_grad, grad_gu[None, None], grad_down[None, None])


def solution(mesh):
    fine = Mesh(mesh.devices.reshape(2, 4, 2, 4, 4, 2), AXES)
    row = P(AXES, None)
    weights = P(SECTION, ("zb", "zo", "yh"), None, None)
    return jax.shard_map(
        per_device,
        mesh=fine,
        in_specs=(row, row, row, row, weights, weights),
        out_specs=(row, row, weights, weights),
        check_vma=False,
    )
```

```python
import functools

import jax
import jax.numpy as jnp
from jax import lax
from jax.experimental import pallas as pl
from jax.experimental.pallas import tpu as pltpu
from jax.sharding import Mesh, PartitionSpec as P

EXPERTS = 4
SECTION = ("ylo", "x", "core")
AXES = ("ylo", "x", "core", "zb", "zo", "yh")
RING = 16
LINE = 4
LANES = 256
BF = jnp.bfloat16
F32 = jnp.float32


def dot(a, b, ca, cb):
    return lax.dot_general(a, b, (((ca,), (cb,)), ((), ())), preferred_element_type=F32)


def up(a):
    return lax.ppermute(a, ("zb", "zo"), [(i, (i + 1) % RING) for i in range(RING)])


def down(a):
    return lax.ppermute(a, ("zb", "zo"), [((i + 1) % RING, i) for i in range(RING)])


def line(a, *pairs):
    return lax.ppermute(a, "zo", pairs)


def across(a):
    return lax.ppermute(a, "yh", [(0, 1), (1, 0)])


def after(a, *others):
    return lax.optimization_barrier((a, *others))[0]


def slice_kernel(cap, zo_ref, gu_ref, g_ref, w_ref, wd_ref, own_ref, other_ref, h_ref, dx_ref):
    rows, hid2 = h_ref.shape
    hidden = hid2 // 2
    padded, width = dx_ref.shape
    pitch = padded // EXPERTS
    gate, upper = gu_ref[:, :hid2], gu_ref[:, hid2:]
    draw = dot(g_ref[...], wd_ref[...], 1, 1)
    sig = jax.nn.sigmoid(gate)
    act = gate * sig
    hid = act * upper
    h_ref[...] = hid.astype(BF)
    dgate = (draw * upper * sig * (1.0 + gate * (1.0 - sig))).astype(BF)
    dupper = (draw * act).astype(BF)
    own_ref[:, :hidden] = dgate[:, :hidden]
    own_ref[:, hidden:] = dupper[:, :hidden]
    other_ref[:, :hidden] = dgate[:, hidden:]
    other_ref[:, hidden:] = dupper[:, hidden:]
    to = lax.broadcasted_iota(jnp.int32, (padded, rows), 0)
    of = lax.broadcasted_iota(jnp.int32, (padded, rows), 1)
    pick = ((to // pitch * cap + to % pitch == of) & (to % pitch < cap)).astype(BF)
    dgu = jnp.concatenate([dgate, dupper], axis=1)
    dgu = dot(pick, dgu, 1, 0).astype(BF)
    dx = dot(dgu, w_ref[...], 1, 1)
    line = lax.dot_general(
        jnp.ones((8, hid2), F32),
        hid * draw,
        (((1,), (1,)), ((), ())),
        preferred_element_type=F32,
        precision=lax.Precision.HIGHEST,
    )
    line = jnp.concatenate([line, jnp.zeros((8, LANES - rows), F32)], axis=1)
    line = jnp.concatenate([line] * (width // LANES), axis=1)[:1]
    lane = lax.broadcasted_iota(jnp.int32, (1, width), 1)
    line = jnp.where(lane // LANES == zo_ref[0], line, 0.0)
    row = lax.broadcasted_iota(jnp.int32, (padded, width), 0)
    dx_ref[...] = jnp.where(row % pitch == cap, line, dx).astype(BF)


def slice_backward(cap, zo, gu, g, w, wd):
    rows, width = g.shape
    hid2 = wd.shape[0]
    whole = pl.BlockSpec(memory_space=pltpu.VMEM)
    return pl.pallas_call(
        functools.partial(slice_kernel, cap),
        out_shape=(
            jax.ShapeDtypeStruct((rows, hid2), BF),
            jax.ShapeDtypeStruct((rows, hid2), BF),
            jax.ShapeDtypeStruct((rows, hid2), BF),
            jax.ShapeDtypeStruct((EXPERTS * (cap + 4), width), BF),
        ),
        in_specs=[pl.BlockSpec(memory_space=pltpu.SMEM)] + [whole] * 4,
        out_specs=(whole,) * 4,
        compiler_params=pltpu.CompilerParams(vmem_limit_bytes=32 * 2**20),
        cost_estimate=pl.CostEstimate(
            flops=2 * rows * width * 3 * hid2, bytes_accessed=5 * 2**20, transcendentals=0
        ),
    )(zo, gu, g, w, wd)


def per_device(tokens, upstream, expert_ids, combine, w_gate_up, w_down):
    tok, width = tokens.shape
    cap = tok * 9 // (8 * EXPERTS)
    pitch = cap + 4
    wgu = w_gate_up[0, 0]
    wdown = w_down[0, 0]
    hidden = wdown.shape[0]
    zb, zo = lax.axis_index("zb"), lax.axis_index("zo")
    sections = lax.axis_size(SECTION)
    out_grad = lax.ppermute(
        upstream, SECTION, [(i, (i - 1) % sections) for i in range(sections)]
    )

    ids = expert_ids[:, 0]
    onehot = (ids[:, None] == jnp.arange(EXPERTS, dtype=jnp.int32)[None, :]).astype(F32)
    earlier = (jnp.arange(tok)[:, None] > jnp.arange(tok)[None, :]).astype(F32)
    before = dot(earlier, onehot, 1, 0)
    slot = jnp.sum(before * onehot, axis=1).astype(jnp.int32)
    rel = (ids - zb) % EXPERTS
    weight = combine.astype(F32)
    scaled = (weight * out_grad.astype(F32)).astype(BF)
    place = (
        jnp.arange(EXPERTS * cap, dtype=jnp.int32)[:, None]
        == (ids * cap + slot)[None, :]
    ).astype(BF)

    def dispatch(a):
        return dot(place, a, 1, 0).astype(BF).reshape(EXPERTS, cap, width)

    def block(a, k):
        return lax.ppermute(a, "zb", [(i, (i + k) % EXPERTS) for i in range(EXPERTS)])

    where = jnp.where
    first, last, odd = zo == 0, zo == 3, (zo % 2) == 1

    def relay(unit):
        r1, l1 = up(unit), down(unit)
        r2, l2 = up(r1), down(l1)
        r3, l3 = line(r2, (2, 3)), line(l2, (1, 0))
        early = where(odd, l1, r1)
        whole = lambda *others: where(
            first, after(l3, *others), where(last, after(r3, *others), early)
        )
        units = [unit, where(odd, r1, l1), early, where(zo < 2, l2, r2)]
        return units, whole

    from_block = (zb - jnp.arange(EXPERTS)) % EXPERTS

    def to_blocks(a):
        units = lax.all_to_all(dispatch(a), "zb", 0, 0, tiled=True)
        return units[from_block].reshape(-1, width)

    unit_x, unit_g = to_blocks(tokens), to_blocks(scaled)
    wgu_other, wdown_other = across(wgu), across(wdown)
    unit_x, wgu_other = lax.optimization_barrier((unit_x, wgu_other))
    unit_g, wdown_other = lax.optimization_barrier((unit_g, wdown_other))
    parts = [a[:, k : k + hidden] for k in (0, hidden) for a in (wgu, wgu_other)]
    wgu_all = jnp.concatenate(parts, axis=1)
    wdown_all = jnp.concatenate([wdown, wdown_other], axis=0)
    (xs, x3), (gs, g3) = relay(unit_x), relay(unit_g)

    forward = lambda x: dot(x, wgu_all, 1, 0)
    expert = lambda gu, g: slice_backward(cap, zo[None], gu, g, wgu_all, wdown_all)
    gus = [forward(after(xs[k], xs[l])) for k, l in ((0, 1), (1, 3), (2, 3))]
    x3 = x3(*gus)
    gus.append(forward(after(xs[3], gs[1])))
    gu3 = forward(x3)
    early = (x3, x3, x3, gs[3])
    done = [expert(gu, after(g, e)) for gu, g, e in zip(gus, gs, early)]

    add = lambda *terms: sum(a.astype(F32) for a in terms).astype(BF)
    d0, d1, d3_early, d2 = (d[3] for d in done)
    r2, l2 = line(d2, (0, 1), (1, 2)), line(d2, (3, 2), (2, 1))
    to_r1 = add(where(zo == 1, d3_early, d1), r2)
    to_l1 = add(where(zo == 2, d3_early, d1), l2)
    r1 = line(to_r1, (0, 1), (1, 2), (2, 3))
    l1 = line(to_l1, (3, 2), (2, 1), (1, 0))
    g3 = g3(to_r1, to_l1, gu3)
    done[2] = expert(gu3, g3)
    far = line(done[2][3], (0, 3), (3, 0))
    own, other, hids, _ = zip(*(done[k] for k in (0, 1, 3, 2)))

    cat = lambda arrays: jnp.concatenate(arrays, axis=0)
    x_all, g_all = cat([xs[0], xs[1], xs[3], x3]), cat([gs[0], gs[1], gs[3], g3])
    hid_all = cat(hids)
    other_gu = dot(x_all, cat(other), 0, 0).astype(BF)
    other_down = dot(hid_all[:, hidden:], g_all, 0, 0).astype(BF)

    other_down = across(other_down)
    dx = add(d0, r1, l1, after(far, other_gu, other_down))
    dx = dx.reshape(EXPERTS, pitch, width)
    far, up1, down1 = (block(dx[k], -k) for k in (2, 1, 3))
    back = jnp.concatenate([dx[0], up1, far, down1], axis=0)
    other_gu = across(other_gu)
    own_gu = lax.optimization_barrier(dot(x_all, cat(own), 0, 0))
    grad_gu = (own_gu + other_gu.astype(F32)).astype(BF)
    grad_down = dot(hid_all[:, :hidden], g_all, 0, 0) + other_down.astype(F32)
    grad_down = grad_down.astype(BF)
    back, grad_gu, grad_down = lax.optimization_barrier((back, grad_gu, grad_down))

    put = (
        jnp.arange(EXPERTS * pitch, dtype=jnp.int32)[:, None]
        == (rel * pitch + slot)[None, :]
    ).astype(BF)
    moe = dot(put, back, 0, 0)
    input_grad = (out_grad.astype(F32) + moe).astype(BF)
    dp = back.reshape(EXPERTS, pitch, width)[:, cap, : LINE * LANES].astype(F32)
    dp = jnp.sum(dp.reshape(EXPERTS, LINE, LANES), axis=1)
    pick = (rel[:, None] == jnp.arange(EXPERTS)[None, :])[:, :, None] & (
        (rel * cap + slot)[:, None] == jnp.arange(LANES)[None, :]
    )[:, None, :]
    dp = jnp.sum(jnp.where(pick, dp[None], 0.0), axis=(1, 2))
    combine_grad = (dp[:, None] / weight).astype(BF)

    return (input_grad, combine_grad, grad_gu[None, None], grad_down[None, None])


def solution(mesh):
    fine = Mesh(mesh.devices.reshape(2, 4, 2, 4, 4, 2), AXES)
    row = P(AXES, None)
    weights = P(SECTION, ("zb", "zo", "yh"), None, None)
    return jax.shard_map(
        per_device,
        mesh=fine,
        in_specs=(row, row, row, row, weights, weights),
        out_specs=(row, row, weights, weights),
        check_vma=False,
    )
```

```python
import functools

import jax
import jax.numpy as jnp
from jax import lax
from jax.experimental import pallas as pl
from jax.experimental.pallas import tpu as pltpu
from jax.sharding import Mesh, PartitionSpec as P

EXPERTS = 4
SECTION = ("ylo", "x", "core")
AXES = ("ylo", "x", "core", "zb", "zo", "yh")
RING = 16
LINE = 4
LANES = 256
BF = jnp.bfloat16
F32 = jnp.float32


def dot(a, b, ca, cb):
    return lax.dot_general(a, b, (((ca,), (cb,)), ((), ())), preferred_element_type=F32)


def up(a):
    return lax.ppermute(a, ("zb", "zo"), [(i, (i + 1) % RING) for i in range(RING)])


def down(a):
    return lax.ppermute(a, ("zb", "zo"), [((i + 1) % RING, i) for i in range(RING)])


def line(a, *pairs):
    return lax.ppermute(a, "zo", pairs)


def across(a):
    return lax.ppermute(a, "yh", [(0, 1), (1, 0)])


def after(a, *others):
    return lax.optimization_barrier((a, *others))[0]


def slice_kernel(cap, zo_ref, gu_ref, g_ref, w_ref, wd_ref, own_ref, other_ref, h_ref, dx_ref):
    rows, hid2 = h_ref.shape
    hidden = hid2 // 2
    padded, width = dx_ref.shape
    pitch = padded // EXPERTS
    gate, upper = gu_ref[:, :hid2], gu_ref[:, hid2:]
    draw = dot(g_ref[...], wd_ref[...], 1, 1)
    sig = jax.nn.sigmoid(gate)
    act = gate * sig
    hid = act * upper
    h_ref[...] = hid.astype(BF)
    dgate = (draw * upper * sig * (1.0 + gate * (1.0 - sig))).astype(BF)
    dupper = (draw * act).astype(BF)
    own_ref[:, :hidden] = dgate[:, :hidden]
    own_ref[:, hidden:] = dupper[:, :hidden]
    other_ref[:, :hidden] = dgate[:, hidden:]
    other_ref[:, hidden:] = dupper[:, hidden:]
    to = lax.broadcasted_iota(jnp.int32, (padded, rows), 0)
    of = lax.broadcasted_iota(jnp.int32, (padded, rows), 1)
    pick = ((to // pitch * cap + to % pitch == of) & (to % pitch < cap)).astype(BF)
    dgu = jnp.concatenate([dgate, dupper], axis=1)
    dgu = dot(pick, dgu, 1, 0).astype(BF)
    dx = dot(dgu, w_ref[...], 1, 1)
    line = lax.dot_general(
        jnp.ones((8, hid2), F32),
        hid * draw,
        (((1,), (1,)), ((), ())),
        preferred_element_type=F32,
        precision=lax.Precision.HIGHEST,
    )
    line = jnp.concatenate([line, jnp.zeros((8, LANES - rows), F32)], axis=1)
    line = jnp.concatenate([line] * (width // LANES), axis=1)[:1]
    lane = lax.broadcasted_iota(jnp.int32, (1, width), 1)
    line = jnp.where(lane // LANES == zo_ref[0], line, 0.0)
    row = lax.broadcasted_iota(jnp.int32, (padded, width), 0)
    dx_ref[...] = jnp.where(row % pitch == cap, line, dx).astype(BF)


def slice_backward(cap, zo, gu, g, w, wd):
    rows, width = g.shape
    hid2 = wd.shape[0]
    whole = pl.BlockSpec(memory_space=pltpu.VMEM)
    return pl.pallas_call(
        functools.partial(slice_kernel, cap),
        out_shape=(
            jax.ShapeDtypeStruct((rows, hid2), BF),
            jax.ShapeDtypeStruct((rows, hid2), BF),
            jax.ShapeDtypeStruct((rows, hid2), BF),
            jax.ShapeDtypeStruct((EXPERTS * (cap + 4), width), BF),
        ),
        in_specs=[pl.BlockSpec(memory_space=pltpu.SMEM)] + [whole] * 4,
        out_specs=(whole,) * 4,
        compiler_params=pltpu.CompilerParams(vmem_limit_bytes=32 * 2**20),
        cost_estimate=pl.CostEstimate(
            flops=2 * rows * width * 3 * hid2, bytes_accessed=5 * 2**20, transcendentals=0
        ),
    )(zo, gu, g, w, wd)


def per_device(tokens, upstream, expert_ids, combine, w_gate_up, w_down):
    tok, width = tokens.shape
    cap = tok * 9 // (8 * EXPERTS)
    pitch = cap + 4
    wgu = w_gate_up[0, 0]
    wdown = w_down[0, 0]
    hidden = wdown.shape[0]
    zb, zo = lax.axis_index("zb"), lax.axis_index("zo")
    sections = lax.axis_size(SECTION)
    out_grad = lax.ppermute(
        upstream, SECTION, [(i, (i - 1) % sections) for i in range(sections)]
    )

    ids = expert_ids[:, 0]
    onehot = (ids[:, None] == jnp.arange(EXPERTS, dtype=jnp.int32)[None, :]).astype(F32)
    earlier = (jnp.arange(tok)[:, None] > jnp.arange(tok)[None, :]).astype(F32)
    before = dot(earlier, onehot, 1, 0)
    slot = jnp.sum(before * onehot, axis=1).astype(jnp.int32)
    rel = (ids - zb) % EXPERTS
    weight = combine.astype(F32)
    scaled = (weight * out_grad.astype(F32)).astype(BF)
    place = (
        jnp.arange(EXPERTS * cap, dtype=jnp.int32)[:, None]
        == (ids * cap + slot)[None, :]
    ).astype(BF)

    def dispatch(a):
        return dot(place, a, 1, 0).astype(BF).reshape(EXPERTS, cap, width)

    def block(a, k):
        return lax.ppermute(a, "zb", [(i, (i + k) % EXPERTS) for i in range(EXPERTS)])

    where = jnp.where
    first, last, odd = zo == 0, zo == 3, (zo % 2) == 1

    def relay(unit):
        r1, l1 = up(unit), down(unit)
        r2, l2 = up(r1), down(l1)
        r3, l3 = line(r2, (2, 3)), line(l2, (1, 0))
        early = where(odd, l1, r1)
        whole = lambda *others: where(
            first, after(l3, *others), where(last, after(r3, *others), early)
        )
        units = [unit, where(odd, r1, l1), early, where(zo < 2, l2, r2)]
        return units, whole

    from_block = (zb - jnp.arange(EXPERTS)) % EXPERTS

    def to_blocks(a):
        units = lax.all_to_all(dispatch(a), "zb", 0, 0, tiled=True)
        return units[from_block].reshape(-1, width)

    unit_x, unit_g = to_blocks(tokens), to_blocks(scaled)
    wgu_other, wdown_other = across(wgu), across(wdown)
    unit_x, wgu_other = lax.optimization_barrier((unit_x, wgu_other))
    unit_g, wdown_other = lax.optimization_barrier((unit_g, wdown_other))
    parts = [a[:, k : k + hidden] for k in (0, hidden) for a in (wgu, wgu_other)]
    wgu_all = jnp.concatenate(parts, axis=1)
    wdown_all = jnp.concatenate([wdown, wdown_other], axis=0)
    (xs, x3), (gs, g3) = relay(unit_x), relay(unit_g)

    forward = lambda x: dot(x, wgu_all, 1, 0)
    expert = lambda gu, g: slice_backward(cap, zo[None], gu, g, wgu_all, wdown_all)
    gus = [forward(after(xs[k], xs[l])) for k, l in ((0, 1), (1, 3), (2, 3))]
    x3 = x3(*gus)
    gus.append(forward(after(xs[3], gs[1])))
    gu3 = forward(x3)
    early = (x3, x3, x3, gs[3])
    done = [None] + [expert(*a) for a in zip(gus[1:], map(after, gs[1:], early[1:]))]

    add = lambda *terms: sum(a.astype(F32) for a in terms).astype(BF)
    d1, d3_early, d2 = (d[3] for d in done[1:])
    r2, l2 = line(d2, (0, 1), (1, 2)), line(d2, (3, 2), (2, 1))
    to_r1 = add(where(zo == 1, d3_early, d1), r2)
    to_l1 = add(where(zo == 2, d3_early, d1), l2)
    r1 = line(to_r1, (0, 1), (1, 2), (2, 3))
    l1 = line(to_l1, (3, 2), (2, 1), (1, 0))
    g3 = g3(to_r1, to_l1, gu3)
    done[2] = expert(gu3, g3)
    far = line(done[2][3], (0, 3), (3, 0))
    done[0] = expert(gus[0], after(gs[0], to_r1, to_l1))
    d0 = done[0][3]
    own, other, hids, _ = zip(*(done[k] for k in (0, 1, 3, 2)))

    cat = lambda arrays: jnp.concatenate(arrays, axis=0)
    x_all, g_all = cat([xs[0], xs[1], xs[3], x3]), cat([gs[0], gs[1], gs[3], g3])
    hid_all = cat(hids)
    other_gu = dot(x_all, cat(other), 0, 0).astype(BF)
    other_down = dot(hid_all[:, hidden:], g_all, 0, 0).astype(BF)

    dx = add(d0, r1, l1, after(far, other_gu, other_down))
    dx = dx.reshape(EXPERTS, pitch, width)
    far, up1, down1 = (block(dx[k], -k) for k in (2, 1, 3))
    back = jnp.concatenate([dx[0], up1, far, down1], axis=0)
    other_gu, other_down = across(other_gu), across(other_down)
    own_gu = lax.optimization_barrier(dot(after(x_all, dx), cat(own), 0, 0))
    grad_gu = (own_gu + other_gu.astype(F32)).astype(BF)
    grad_down = dot(hid_all[:, :hidden], g_all, 0, 0) + other_down.astype(F32)
    grad_down = grad_down.astype(BF)
    back, grad_gu, grad_down = lax.optimization_barrier((back, grad_gu, grad_down))

    put = (
        jnp.arange(EXPERTS * pitch, dtype=jnp.int32)[:, None]
        == (rel * pitch + slot)[None, :]
    ).astype(BF)
    moe = dot(put, back, 0, 0)
    input_grad = (out_grad.astype(F32) + moe).astype(BF)
    dp = back.reshape(EXPERTS, pitch, width)[:, cap, : LINE * LANES].astype(F32)
    dp = jnp.sum(dp.reshape(EXPERTS, LINE, LANES), axis=1)
    pick = (rel[:, None] == jnp.arange(EXPERTS)[None, :])[:, :, None] & (
        (rel * cap + slot)[:, None] == jnp.arange(LANES)[None, :]
    )[:, None, :]
    dp = jnp.sum(jnp.where(pick, dp[None], 0.0), axis=(1, 2))
    combine_grad = (dp[:, None] / weight).astype(BF)

    return (input_grad, combine_grad, grad_gu[None, None], grad_down[None, None])


def solution(mesh):
    fine = Mesh(mesh.devices.reshape(2, 4, 2, 4, 4, 2), AXES)
    row = P(AXES, None)
    weights = P(SECTION, ("zb", "zo", "yh"), None, None)
    return jax.shard_map(
        per_device,
        mesh=fine,
        in_specs=(row, row, row, row, weights, weights),
        out_specs=(row, row, weights, weights),
        check_vma=False,
    )
```
